1024 devices in a mesh: blk: 32 (over z_lo, x), group: 32 (over z_hi, y, core).
Axes of the slice: x: 4, y: 8, z: 16 (z_hi: 2, z_lo: 8; z = z_hi * 8 + z_lo), core: 2. Of those that a mesh axis runs over, the one named last changes fastest.
Arguments:
- user_factors: float32 [262144, 256], P(('blk', 'group')), may hold values from -1.5 to 1.5
- user_state: float32 [262144, 256], P(('blk', 'group')), may hold values from 0.5 to 20
- item_factors: float32 [262144, 256], P(('blk', 'group')), may hold values from -1.5 to 1.5
- item_state: float32 [262144, 256], P(('blk', 'group')), may hold values from 0.5 to 20
- counts: int32 [262144, 1024], P(('blk', 'group')), may hold values from 0 to 5
Outputs:
- users_out: float32 [262144, 256], P(('blk', 'group'))
- user_state_out: float32 [262144, 256], P(('blk', 'group'))
- items_out: float32 [262144, 256], P(('blk', 'group'))
- item_state_out: float32 [262144, 256], P(('blk', 'group'))
The draws below stay inside these ranges and needn't reach their ends.
All inputs are finite; a program needn't handle non-finite values.
Results may differ from the reference program's by a relative error of at most 0.0003.
Values sent between devices are 32-bit elements; how exact they have to be, the bound alone decides.
A program may use at most 32 MiB of HBM per device.

```python
import math
import jax
import jax.numpy as jnp
from jax import lax

R = 256
USERS_DEV = 256
ITEM_BLK = 256
STRATA = 4
USERS = 262144
ITEMS = 262144
N_BLK = 32
N_GROUP = 32


def plant(entries, stream_key, low, high):
    shape = entries.shape
    index_at = [jax.random.randint(jax.random.fold_in(stream_key, axis), (), 0, shape[axis]) for axis in range(len(shape))]
    entries = entries.at[tuple(index_at)].set(low)
    longest = shape.index(max(shape))
    index_at[longest] = (index_at[longest] + 1) % shape[longest]
    return entries.at[tuple(index_at)].set(high)


def block_scale(stream_key, shape, shards, least, high):
    loudness, own = 1.0, jax.random.fold_in(stream_key, 6)
    for dim, shards_of in shards:
        heights = jnp.exp(jax.random.uniform(jax.random.fold_in(own, dim), (shards_of,), jnp.float32, least / len(shards), high / len(shards)))
        loudness = loudness * jnp.repeat(heights, shape[dim] // shards_of).reshape([-1 if axis == dim else 1 for axis in range(len(shape))])
    return loudness


def centred(own_key, dims, spread, bound, split=(), kind=jnp.bfloat16):
    array = spread * jax.random.normal(own_key, dims, jnp.float32)
    if split:
        array = array * block_scale(own_key, dims, split, -0.22, 0.18)
    return jnp.clip(array, -bound, bound).astype(kind)


def setup_inputs(seed: int = 0) -> dict:
    key_list = jax.random.split(jax.random.key(seed), 6)
    user_factors = centred(key_list[0], (USERS, R), 0.25, 1.5, ((0, 1024),), jnp.float32)
    user_state = jnp.clip(jnp.exp(math.log(20.0) - 3.6888795 * jax.random.uniform(key_list[1], (USERS, R), jnp.float32) ** block_scale(key_list[1], (USERS, R), ((0, 1024),), -0.2, 0.2)), 0.5, 20.0)
    item_factors = centred(key_list[2], (ITEMS, R), 0.25, 1.5, ((0, 1024),), jnp.float32)
    item_state = jnp.clip(jnp.exp(math.log(20.0) - 3.6888795 * jax.random.uniform(key_list[3], (ITEMS, R), jnp.float32) ** block_scale(key_list[3], (ITEMS, R), ((0, 1024),), -0.2, 0.2)), 0.5, 20.0)
    counts = plant(jax.random.randint(key_list[4], (USERS, STRATA * ITEM_BLK), 0, 6), jax.random.fold_in(key_list[4], 1), 0, 5).astype(jnp.int32)
    return dict(user_factors=user_factors, user_state=user_state, item_factors=item_factors, item_state=item_state, counts=counts)


conf_scale = 0.5
ridge_weight = 0.01
step_rate = 0.1

def update_block(users, user_acc, items, item_acc, count_tile):
    highest = lax.Precision.HIGHEST
    predicted = jnp.dot(users, items.T, precision=highest)
    prefer = (count_tile > 0).astype(users.dtype)
    confidence = 1.0 + conf_scale * count_tile.astype(users.dtype)
    weighted_gap = confidence * (predicted - prefer)
    user_grad = 2.0 * jnp.dot(weighted_gap, items, precision=highest) + 2.0 * ridge_weight * users
    item_grad = 2.0 * jnp.dot(weighted_gap.T, users, precision=highest) + 2.0 * ridge_weight * items
    user_acc = user_acc + user_grad * user_grad
    item_acc = item_acc + item_grad * item_grad
    users = users - step_rate * user_grad / jnp.sqrt(user_acc)
    items = items - step_rate * item_grad / jnp.sqrt(item_acc)
    return (users, user_acc, items, item_acc)

def per_blk(packed):
    return jax.vmap(update_block)(*packed)

def reference(user_factors, user_state, item_factors, item_state, counts):
    users = user_factors.reshape(N_BLK, N_GROUP, USERS_DEV, R)
    user_acc = user_state.reshape(N_BLK, N_GROUP, USERS_DEV, R)
    items = item_factors.reshape(N_BLK, N_GROUP, ITEM_BLK, R)
    item_acc = item_state.reshape(N_BLK, N_GROUP, ITEM_BLK, R)
    count_grid = counts.reshape(N_BLK, N_GROUP, USERS_DEV, STRATA, ITEM_BLK)
    for stratum in range(STRATA):
        count_tile = count_grid[:, :, :, stratum, :]
        users, user_acc, items, item_acc = lax.map(per_blk, (users, user_acc, items, item_acc, count_tile))
        items = jnp.roll(items, 1, axis=0)
        item_acc = jnp.roll(item_acc, 1, axis=0)
    items = jnp.roll(items, 1, axis=1)
    item_acc = jnp.roll(item_acc, 1, axis=1)
    return (users.reshape(USERS, R), user_acc.reshape(USERS, R), items.reshape(ITEMS, R), item_acc.reshape(ITEMS, R))
```

```python
import functools
import jax
import jax.numpy as jnp
from jax import lax
from jax.experimental import pallas as pl
from jax.experimental.pallas import tpu as pltpu
from jax.sharding import PartitionSpec as P

STRATA = 4
R = 256
XS = 4
NC = 4
CH = R // NC
MESH = pl.DeviceIdType.MESH

conf_scale = 0.5
ridge_weight = 0.01
step_rate = 0.1

NT = (((1,), (1,)), ((), ()))
NN = (((1,), (0,)), ((), ()))
TN = (((0,), (0,)), ((), ()))


def split(value):
    high = value.astype(jnp.bfloat16)
    return high, (value - high.astype(jnp.float32)).astype(jnp.bfloat16)


def dot3(left, right, dims):
    (lh, ll), (rh, rl) = left, right
    dot = functools.partial(lax.dot_general, dimension_numbers=dims, preferred_element_type=jnp.float32)
    return dot(lh, rh) + (dot(lh, rl) + dot(ll, rh))


def weigh(counts, predicted):
    prefer = (counts > 0).astype(jnp.float32)
    return (1.0 + conf_scale * counts) * (predicted - prefer)


def adagrad(value, acc, grad):
    acc = acc + grad * grad
    return value - step_rate * grad * lax.rsqrt(acc), acc


def kernel(n_blk, n_group, u_in, a_in, v_in, b_in, k_in, u_out, a_out, v_out, b_out,
           users, user_acc, home_v, home_b, kraw, kt, vin, gin, gout, uh, ul, vh, vl, gh, gl,
           load, store, vsend, vrecv, gsend, grecv, msend, mrecv, fsend, frecv):
    b, g = lax.axis_index("blk"), lax.axis_index("group")
    x = lax.rem(b, XS)
    plane = b - x

    def at(blk, group=g):
        return {"blk": blk, "group": group}

    def ring(steps):
        return at(plane + lax.rem(x + steps, XS))

    nxt, prv = lax.rem(b + XS, n_blk), lax.rem(b + n_blk - XS, n_blk)
    final = at(jnp.where(x == 0, nxt, b), lax.rem(g + 1, n_group))
    final_from = at(jnp.where(x == 0, prv, b), lax.rem(g + n_group - 1, n_group))

    loads = [
        pltpu.make_async_copy(u_in, users, load.at[0]),
        pltpu.make_async_copy(v_in, home_v.at[0], load.at[1]),
        pltpu.make_async_copy(k_in, kraw, load.at[2]),
        pltpu.make_async_copy(b_in, home_b.at[0], load.at[3]),
        pltpu.make_async_copy(a_in, user_acc, load.at[4]),
    ]
    for copy in loads:
        copy.start()
    barrier = pltpu.get_barrier_semaphore()
    for device in (ring(1), ring(2), ring(3), at(nxt), at(prv), final, final_from):
        pl.semaphore_signal(barrier, inc=1, device_id=device, device_id_type=MESH)

    def rows(k):
        return pl.ds(k * CH, CH)

    def slot(s):
        return (x >= XS - s).astype(jnp.int32)

    def v_copy(s, k):
        return pltpu.make_async_remote_copy(
            home_v.at[slot(s), rows(k)], vin.at[s - 1, rows(k)], vsend.at[s - 1, k], vrecv.at[s - 1, k],
            device_id=ring(s), device_id_type=MESH)

    def g_copy(s, k):
        return pltpu.make_async_remote_copy(
            gout.at[s - 1, rows(k)], gin.at[s - 1, rows(k)], gsend.at[s - 1, k], grecv.at[s - 1, k],
            device_id=ring(XS - s), device_id_type=MESH)

    def m_copy(which, k):
        ref = (home_v, home_b)[which]
        return pltpu.make_async_remote_copy(
            ref.at[0, rows(k)], ref.at[1, rows(k)], msend.at[which, k], mrecv.at[which, k],
            device_id=at(nxt), device_id_type=MESH)

    def f_copy(which, k):
        ref, out = ((home_v, v_out), (home_b, b_out))[which]
        return pltpu.make_async_remote_copy(
            ref.at[slot(3), rows(k)], out.at[rows(k)], fsend.at[which, k], frecv.at[which, k],
            device_id=final, device_id_type=MESH)

    def send_v(s, k):
        @pl.when(x == XS - s)
        def _():
            m_copy(0, k).start()

        @pl.when(x != XS - s)
        def _():
            v_copy(s, k).start()

    def send_b(s):
        @pl.when(x == XS - s)
        def _():
            for k in range(NC):
                m_copy(1, k).start()

    def update_users(grad):
        grad = 2.0 * grad + (2.0 * ridge_weight) * users[...]
        users[...], user_acc[...] = adagrad(users[...], user_acc[...], grad)
        uh[...], ul[...] = split(users[...])

    loads[0].wait()
    uh[...], ul[...] = split(users[...])
    loads[1].wait()
    vh[...], vl[...] = split(home_v[0])
    loads[2].wait()
    usplit, vsplit = (uh[...], ul[...]), (vh[...], vl[...])
    gap = split(weigh(kraw[:, :R].astype(jnp.float32), dot3(usplit, vsplit, NT)))
    grad = 2.0 * dot3(gap, usplit, TN) + (2.0 * ridge_weight) * home_v[0]
    loads[3].wait()
    home_v[0], home_b[0] = adagrad(home_v[0], home_b[0], grad)
    pl.semaphore_wait(barrier, 7)
    for k in range(NC):
        send_v(1, k)
    send_b(1)
    loads[4].wait()
    update_users(dot3(gap, vsplit, NN))
    for s in range(1, STRATA):
        kt[s - 1] = kraw[:, s * R : (s + 1) * R].astype(jnp.float32).T

    for s in range(1, STRATA):
        for k in range(NC):
            @pl.when(x == XS - s)
            def _():
                m_copy(0, k).wait_recv()
                v_copy(s, k).start()

            v_copy(s, k).wait_recv()
            items = vin[s - 1, rows(k)]
            items_split = split(items)
            vh[rows(k)], vl[rows(k)] = items_split
            usplit = (uh[...], ul[...])
            gap = split(weigh(kt[s - 1, rows(k)], dot3(items_split, usplit, NT)))
            gh[rows(k)], gl[rows(k)] = gap
            gout[s - 1, rows(k)] = 2.0 * dot3(gap, usplit, NN) + (2.0 * ridge_weight) * items
            g_copy(s, k).start()
        update_users(dot3((gh[...], gl[...]), (vh[...], vl[...]), TN))
        if s == STRATA - 1:
            stores = [pltpu.make_async_copy(users, u_out, store.at[0]), pltpu.make_async_copy(user_acc, a_out, store.at[1])]
            for copy in stores:
                copy.start()
        for k in range(NC):
            @pl.when(x == XS - s)
            def _():
                m_copy(1, k).wait_recv()

            v_copy(s, k).wait_send()
            g_copy(s, k).wait_recv()
            now = slot(s)
            home_v[now, rows(k)], home_b[now, rows(k)] = adagrad(home_v[now, rows(k)], home_b[now, rows(k)], gin[s - 1, rows(k)])
            if s < STRATA - 1:
                send_v(s + 1, k)
            else:
                f_copy(0, k).start()
                f_copy(1, k).start()
        if s < STRATA - 1:
            send_b(s + 1)

    for s in range(1, STRATA):
        for k in range(NC):
            g_copy(s, k).wait_send()

    @pl.when(x != 0)
    def _():
        for which in range(2):
            for k in range(NC):
                m_copy(which, k).wait_send()

    for which in range(2):
        for k in range(NC):
            f_copy(which, k).wait()
    for copy in stores:
        copy.wait()


def body(user_factors, user_state, item_factors, item_state, counts):
    anywhere = pl.BlockSpec(memory_space=pl.ANY)
    block = jax.ShapeDtypeStruct((R, R), jnp.float32)
    f32, bf16 = jnp.float32, jnp.bfloat16
    dma = pltpu.SemaphoreType.DMA
    return pl.pallas_call(
        functools.partial(kernel, lax.axis_size("blk"), lax.axis_size("group")),
        out_shape=(block,) * 4,
        in_specs=[anywhere] * 5,
        out_specs=(anywhere,) * 4,
        scratch_shapes=[
            pltpu.VMEM((R, R), f32), pltpu.VMEM((R, R), f32),
            pltpu.VMEM((2, R, R), f32), pltpu.VMEM((2, R, R), f32),
            pltpu.VMEM((R, STRATA * R), jnp.int32), pltpu.VMEM((3, R, R), f32),
            pltpu.VMEM((3, R, R), f32), pltpu.VMEM((3, R, R), f32), pltpu.VMEM((3, R, R), f32),
            pltpu.VMEM((R, R), bf16), pltpu.VMEM((R, R), bf16),
            pltpu.VMEM((R, R), bf16), pltpu.VMEM((R, R), bf16),
            pltpu.VMEM((R, R), bf16), pltpu.VMEM((R, R), bf16),
            dma((5,)), dma((2,)),
            dma((3, NC)), dma((3, NC)), dma((3, NC)), dma((3, NC)),
            dma((2, NC)), dma((2, NC)), dma((2, NC)), dma((2, NC)),
        ],
        compiler_params=pltpu.CompilerParams(collective_id=0, has_side_effects=True, vmem_limit_bytes=32 * 2**20),
        name="strata",
    )(user_factors, user_state, item_factors, item_state, counts)


def solution(mesh):
    spec = P(("blk", "group"), None)
    return jax.shard_map(body, mesh=mesh, in_specs=(spec,) * 5, out_specs=(spec,) * 4, check_vma=False)
```

```python
import functools
import jax
import jax.numpy as jnp
from jax import lax
from jax.experimental import pallas as pl
from jax.experimental.pallas import tpu as pltpu
from jax.sharding import PartitionSpec as P

STRATA = 4
R = 256
XS = 4
YC = 16
NC = 4
CH = R // NC
HALF = NC // 2
MESH = pl.DeviceIdType.MESH

conf_scale = 0.5
ridge_weight = 0.01
step_rate = 0.1

NT = (((1,), (1,)), ((), ()))
NN = (((1,), (0,)), ((), ()))
TN = (((0,), (0,)), ((), ()))


def split(value):
    high = value.astype(jnp.bfloat16)
    return high, (value - high.astype(jnp.float32)).astype(jnp.bfloat16)


def dot3(left, right, dims):
    (lh, ll), (rh, rl) = left, right
    dot = functools.partial(lax.dot_general, dimension_numbers=dims, preferred_element_type=jnp.float32)
    return dot(lh, rh) + (dot(lh, rl) + dot(ll, rh))


def weigh(counts, predicted):
    prefer = (counts > 0).astype(jnp.float32)
    return (1.0 + conf_scale * counts) * (predicted - prefer)


def adagrad(value, acc, grad):
    acc = acc + grad * grad
    return value - step_rate * grad * lax.rsqrt(acc), acc


def kernel(n_blk, n_group, u_in, a_in, v_in, b_in, k_in, u_out, a_out, v_out, b_out,
           users, user_acc, home_v, home_b, kraw, kt, vin, gin, gout, uh, ul, vh, vl, gh, gl,
           relay, load, store, vsend, vrecv, gsend, grecv, msend, mrecv, fsend, frecv, lsend, lrecv):
    b, g = lax.axis_index("blk"), lax.axis_index("group")
    x = lax.rem(b, XS)
    plane = b - x

    def at(blk, group=g):
        return {"blk": blk, "group": group}

    def ring(steps):
        return at(plane + lax.rem(x + steps, XS))

    nxt, prv = lax.rem(b + XS, n_blk), lax.rem(b + n_blk - XS, n_blk)
    to_blk, from_blk = jnp.where(x == 0, nxt, b), jnp.where(x == 0, prv, b)
    final = at(to_blk, lax.rem(g + 1, n_group))
    final_from = at(from_blk, lax.rem(g + n_group - 1, n_group))
    first, last = lax.rem(g, YC) == 0, lax.rem(g, YC) == YC - 1
    across = at(b, lax.rem(g + YC, n_group))
    beside = at(to_blk, lax.rem(g + YC + 1, n_group))
    barrier = pltpu.get_barrier_semaphore()

    def greet(device):
        pl.semaphore_signal(barrier, inc=1, device_id=device, device_id_type=MESH)

    loads = [
        pltpu.make_async_copy(u_in, users, load.at[0]),
        pltpu.make_async_copy(v_in, home_v.at[0], load.at[1]),
        pltpu.make_async_copy(k_in, kraw, load.at[2]),
        pltpu.make_async_copy(b_in, home_b.at[0], load.at[3]),
        pltpu.make_async_copy(a_in, user_acc, load.at[4]),
    ]
    for copy in loads:
        copy.start()
    for device in (ring(1), ring(2), ring(3)):
        greet(device)

    @pl.when(x != 0)
    def _():
        greet(at(prv))

    @pl.when(jnp.logical_not(first))
    def _():
        greet(final_from)

    @pl.when(first | last)
    def _():
        greet(across)

    @pl.when(first)
    def _():
        greet(at(from_blk, lax.rem(g + n_group - YC - 1, n_group)))

    def rows(k):
        return pl.ds(k * CH, CH)

    def slot(s):
        return (x >= XS - s).astype(jnp.int32)

    def v_copy(s, k):
        return pltpu.make_async_remote_copy(
            home_v.at[slot(s), rows(k)], vin.at[s - 1, rows(k)], vsend.at[s - 1, k], vrecv.at[s - 1, k],
            device_id=ring(s), device_id_type=MESH)

    def g_copy(s, k):
        return pltpu.make_async_remote_copy(
            gout.at[s - 1, rows(k)], gin.at[s - 1, rows(k)], gsend.at[s - 1, k], grecv.at[s - 1, k],
            device_id=ring(XS - s), device_id_type=MESH)

    def m_copy(which, k):
        ref = (home_v, home_b)[which]
        return pltpu.make_async_remote_copy(
            ref.at[0, rows(k)], ref.at[1, rows(k)], msend.at[which, k], mrecv.at[which, k],
            device_id=at(nxt), device_id_type=MESH)

    def f_copy(which, k):
        ref, out = ((home_v, v_out), (home_b, b_out))[which]
        return pltpu.make_async_remote_copy(
            ref.at[slot(3), rows(k)], out.at[rows(k)], fsend.at[which, k], frecv.at[which, k],
            device_id=final, device_id_type=MESH)

    def first_leg(which, k):
        ref = (home_v, home_b)[which]
        return pltpu.make_async_remote_copy(
            ref.at[slot(3), rows(k)], relay.at[which, rows(k % HALF)], fsend.at[which, k], lrecv.at[which, k % HALF],
            device_id=across if k < HALF else beside, device_id_type=MESH)

    def second_leg(which, k):
        out = (v_out, b_out)[which]
        return pltpu.make_async_remote_copy(
            relay.at[which, rows(k % HALF)], out.at[rows(k)], lsend.at[which, k % HALF], frecv.at[which, k],
            device_id=beside if k < HALF else across, device_id_type=MESH)

    def send_v(s, k):
        @pl.when(x == XS - s)
        def _():
            m_copy(0, k).start()

        @pl.when(x != XS - s)
        def _():
            v_copy(s, k).start()

    def send_b(s):
        @pl.when(x == XS - s)
        def _():
            for k in range(NC):
                m_copy(1, k).start()

    def update_users(grad):
        grad = 2.0 * grad + (2.0 * ridge_weight) * users[...]
        users[...], user_acc[...] = adagrad(users[...], user_acc[...], grad)
        uh[...], ul[...] = split(users[...])

    loads[0].wait()
    uh[...], ul[...] = split(users[...])
    loads[1].wait()
    vh[...], vl[...] = split(home_v[0])
    loads[2].wait()
    usplit, vsplit = (uh[...], ul[...]), (vh[...], vl[...])
    gap = split(weigh(kraw[:, :R].astype(jnp.float32), dot3(usplit, vsplit, NT)))
    grad = 2.0 * dot3(gap, usplit, TN) + (2.0 * ridge_weight) * home_v[0]
    loads[3].wait()
    home_v[0], home_b[0] = adagrad(home_v[0], home_b[0], grad)
    pl.semaphore_wait(barrier, 4 + (x != 0).astype(jnp.int32) + (first | last).astype(jnp.int32))
    for k in range(NC):
        send_v(1, k)
    send_b(1)
    loads[4].wait()
    update_users(dot3(gap, vsplit, NN))
    for s in range(1, STRATA):
        kt[s - 1] = kraw[:, s * R : (s + 1) * R].astype(jnp.float32).T

    for s in range(1, STRATA):
        for k in range(NC):
            @pl.when(x == XS - s)
            def _():
                m_copy(0, k).wait_recv()
                v_copy(s, k).start()

            v_copy(s, k).wait_recv()
            items = vin[s - 1, rows(k)]
            items_split = split(items)
            vh[rows(k)], vl[rows(k)] = items_split
            usplit = (uh[...], ul[...])
            gap = split(weigh(kt[s - 1, rows(k)], dot3(items_split, usplit, NT)))
            gh[rows(k)], gl[rows(k)] = gap
            gout[s - 1, rows(k)] = 2.0 * dot3(gap, usplit, NN) + (2.0 * ridge_weight) * items
            g_copy(s, k).start()
        update_users(dot3((gh[...], gl[...]), (vh[...], vl[...]), TN))
        if s == STRATA - 1:
            stores = [pltpu.make_async_copy(users, u_out, store.at[0]), pltpu.make_async_copy(user_acc, a_out, store.at[1])]
            for copy in stores:
                copy.start()
        for k in range(NC):
            @pl.when(x == XS - s)
            def _():
                m_copy(1, k).wait_recv()

            v_copy(s, k).wait_send()
            g_copy(s, k).wait_recv()
            now = slot(s)
            home_v[now, rows(k)], home_b[now, rows(k)] = adagrad(home_v[now, rows(k)], home_b[now, rows(k)], gin[s - 1, rows(k)])
            if s < STRATA - 1:
                send_v(s + 1, k)
            else:
                @pl.when(last)
                def _():
                    first_leg(0, k).start()
                    first_leg(1, k).start()

                @pl.when(jnp.logical_not(last))
                def _():
                    f_copy(0, k).start()
                    f_copy(1, k).start()
        if s < STRATA - 1:
            send_b(s + 1)

    for s in range(1, STRATA):
        for k in range(NC):
            g_copy(s, k).wait_send()

    @pl.when(x != 0)
    def _():
        for which in range(2):
            for k in range(NC):
                m_copy(which, k).wait_send()

    for role, chunks in ((last, range(HALF)), (first, range(HALF, NC))):
        @pl.when(role)
        def _():
            for k in chunks:
                for which in range(2):
                    first_leg(which, k).wait_recv()
                    second_leg(which, k).start()
            for k in chunks:
                for which in range(2):
                    second_leg(which, k).wait_send()

    for which in range(2):
        for k in range(NC):
            f_copy(which, k).wait()
    for copy in stores:
        copy.wait()


def body(user_factors, user_state, item_factors, item_state, counts):
    anywhere = pl.BlockSpec(memory_space=pl.ANY)
    block = jax.ShapeDtypeStruct((R, R), jnp.float32)
    f32, bf16 = jnp.float32, jnp.bfloat16
    dma = pltpu.SemaphoreType.DMA
    return pl.pallas_call(
        functools.partial(kernel, lax.axis_size("blk"), lax.axis_size("group")),
        out_shape=(block,) * 4,
        in_specs=[anywhere] * 5,
        out_specs=(anywhere,) * 4,
        scratch_shapes=[
            pltpu.VMEM((R, R), f32), pltpu.VMEM((R, R), f32),
            pltpu.VMEM((2, R, R), f32), pltpu.VMEM((2, R, R), f32),
            pltpu.VMEM((R, STRATA * R), jnp.int32), pltpu.VMEM((3, R, R), f32),
            pltpu.VMEM((3, R, R), f32), pltpu.VMEM((3, R, R), f32), pltpu.VMEM((3, R, R), f32),
            pltpu.VMEM((R, R), bf16), pltpu.VMEM((R, R), bf16),
            pltpu.VMEM((R, R), bf16), pltpu.VMEM((R, R), bf16),
            pltpu.VMEM((R, R), bf16), pltpu.VMEM((R, R), bf16),
            pltpu.VMEM((2, R // 2, R), f32),
            dma((5,)), dma((2,)),
            dma((3, NC)), dma((3, NC)), dma((3, NC)), dma((3, NC)),
            dma((2, NC)), dma((2, NC)), dma((2, NC)), dma((2, NC)), dma((2, HALF)), dma((2, HALF)),
        ],
        compiler_params=pltpu.CompilerParams(collective_id=0, has_side_effects=True, vmem_limit_bytes=60 * 2**20),
        name="strata",
    )(user_factors, user_state, item_factors, item_state, counts)


def solution(mesh):
    spec = P(("blk", "group"), None)
    return jax.shard_map(body, mesh=mesh, in_specs=(spec,) * 5, out_specs=(spec,) * 4, check_vma=False)
```

```python
import functools
import jax
import jax.numpy as jnp
from jax import lax
from jax.experimental import pallas as pl
from jax.experimental.pallas import tpu as pltpu
from jax.sharding import PartitionSpec as P

STRATA = 4
R = 256
XS = 4
YC = 16
NC = 4
CH = R // NC
LANES = (1, 3, 5, 7, 9, 11, 13, 14)
NP = len(LANES)
PIECE = R // NP
MESH = pl.DeviceIdType.MESH

conf_scale = 0.5
ridge_weight = 0.01
step_rate = 0.1

NT = (((1,), (1,)), ((), ()))
NN = (((1,), (0,)), ((), ()))
TN = (((0,), (0,)), ((), ()))


def split(value):
    high = value.astype(jnp.bfloat16)
    return high, (value - high.astype(jnp.float32)).astype(jnp.bfloat16)


def dot3(left, right, dims):
    (lh, ll), (rh, rl) = left, right
    dot = functools.partial(lax.dot_general, dimension_numbers=dims, preferred_element_type=jnp.float32)
    return dot(lh, rh) + (dot(lh, rl) + dot(ll, rh))


def weigh(counts, predicted):
    prefer = (counts > 0).astype(jnp.float32)
    return (1.0 + conf_scale * counts) * (predicted - prefer)


def adagrad(value, acc, grad):
    acc = acc + grad * grad
    return value - step_rate * grad * lax.rsqrt(acc), acc


def kernel(n_blk, n_group, u_in, a_in, v_in, b_in, k_in, u_out, a_out, e_out, v_out, b_out, g_out,
           users, user_acc, user_grad, home_v, home_b, kraw, kt, vin, gin, gout, uh, ul, vh, vl, gh, gl, relay, far, far_grad,
           load, store, vsend, vrecv, gsend, grecv, msend, mrecv, fsend, frecv, asend, arecv, zsend, zrecv, far_store):
    b, g = lax.axis_index("blk"), lax.axis_index("group")
    x = lax.rem(b, XS)
    plane = b - x

    def at(blk, group=g):
        return {"blk": blk, "group": group}

    def moved(blk_steps, group_steps=0):
        return at(lax.rem(b + blk_steps + n_blk, n_blk), lax.rem(g + group_steps + n_group, n_group))

    def ring(steps):
        return at(plane + lax.rem(x + steps, XS))

    def flag(condition):
        return condition.astype(jnp.int32)

    nxt, prv = moved(XS), moved(-XS)
    gone = jnp.where(x <= 1, XS, 0)
    lane = lax.rem(g, YC)
    first, last = lane == 0, lane == YC - 1
    relays = [lane == other for other in LANES]
    relaying = functools.reduce(jnp.logical_or, relays)

    loads = [
        pltpu.make_async_copy(u_in, users, load.at[0]),
        pltpu.make_async_copy(v_in, home_v.at[0], load.at[1]),
        pltpu.make_async_copy(k_in, kraw, load.at[2]),
        pltpu.make_async_copy(b_in, home_b.at[0], load.at[3]),
        pltpu.make_async_copy(a_in, user_acc, load.at[4]),
    ]
    for copy in loads:
        copy.start()

    barrier = pltpu.get_barrier_semaphore()

    def greet(*devices):
        for device in devices:
            pl.semaphore_signal(barrier, inc=1, device_id=device, device_id_type=MESH)

    greet(ring(1), ring(2), ring(3))

    @pl.when(x == 0)
    def _():
        greet(moved(1 - XS), moved(2 - XS), moved(3 - XS))

    @pl.when(x >= 2)
    def _():
        greet(prv)

    @pl.when(jnp.logical_not(first))
    def _():
        greet(moved(-gone, -1), moved(-1, -1))

    @pl.when(first)
    def _():
        greet(*[moved(-gone, other - YC) for other in LANES])

    @pl.when(first & (x == 1))
    def _():
        greet(*[moved(0, other - YC) for other in LANES])

    @pl.when(relaying)
    def _():
        greet(at(b, g - lane + YC - 1), at(plane + lax.rem(x + XS - 1, XS), g - lane + YC - 1))

    def rows(k):
        return pl.ds(k * CH, CH)

    def slot(s):
        return flag(x >= XS - s)

    def remote(src, dst, send, recv, device):
        return pltpu.make_async_remote_copy(src, dst, send, recv, device_id=device, device_id_type=MESH)

    def v_copy(s, k, device=None):
        return remote(home_v.at[slot(s - 1), rows(k)], vin.at[s - 1, rows(k)], vsend.at[s - 1, k], vrecv.at[s - 1, k],
                      ring(s) if device is None else device)

    def g_copy(s, k):
        return remote(gout.at[s - 1, rows(k)], gin.at[s - 1, rows(k)], gsend.at[s - 1, k], grecv.at[s - 1, k], ring(XS - s))

    def m_copy(which, k):
        ref = (home_v, home_b)[which]
        return remote(ref.at[0, rows(k)], ref.at[1, rows(k)], msend.at[which, k], mrecv.at[which, k], nxt)

    def home_rows(which, k):
        return (home_v, home_b)[which].at[slot(2), rows(k)]

    def steps(which):
        return 1 if which >= 2 else gone

    def f_copy(which, k):
        src = gout.at[2, rows(k)] if which == 2 else home_rows(which, k)
        return remote(src, (v_out, b_out, g_out)[which].at[rows(k)], fsend.at[which, k], frecv.at[which, k],
                      moved(steps(which), 1))

    def part(p):
        return pl.ds(p * PIECE, PIECE)

    def first_leg(which, p):
        src = ((home_v, home_b)[which].at[slot(2), part(p)] if which < 2 else
               users.at[part(p)] if which == 2 else kt.at[2, part(p)])
        return remote(src, relay.at[which], zsend.at[which, p], arecv.at[which], at(b if which < 2 else plane + lax.rem(x + 1, XS), g + LANES[p] - YC + 1))

    def last_leg(which, p):
        return remote(relay.at[which], far.at[which, part(p)], asend.at[which], zrecv.at[which, p],
                      moved(gone if which < 2 else jnp.where(x == 0, XS, 0), YC - LANES[p]))

    def send_far(which):
        for p in range(NP):
            first_leg(which, p).start()

    def pass_on(arrays):
        for role, p in zip(relays, range(NP)):
            @pl.when(role)
            def _():
                for which in arrays:
                    first_leg(which, p).wait_recv()
                    last_leg(which, p).start()

    def send_v(s, k):
        @pl.when(x == XS - s)
        def _():
            v_copy(s, k, moved(s)).start()

        @pl.when(x != XS - s)
        def _():
            v_copy(s, k).start()

    def migrate(s):
        @pl.when(x == XS - s)
        def _():
            for k in range(NC):
                m_copy(0, k).start()
                m_copy(1, k).start()

    def user_gradient(grad):
        return 2.0 * grad + (2.0 * ridge_weight) * users[...]

    def update_users(grad):
        users[...], user_acc[...] = adagrad(users[...], user_acc[...], user_gradient(grad))
        uh[...], ul[...] = split(users[...])

    loads[0].wait()
    uh[...], ul[...] = split(users[...])
    loads[1].wait()
    vh[...], vl[...] = split(home_v[0])
    loads[2].wait()
    usplit, vsplit = (uh[...], ul[...]), (vh[...], vl[...])
    gap = split(weigh(kraw[:, :R].astype(jnp.float32), dot3(usplit, vsplit, NT)))
    grad = 2.0 * dot3(gap, usplit, TN) + (2.0 * ridge_weight) * home_v[0]
    loads[3].wait()
    home_v[0], home_b[0] = adagrad(home_v[0], home_b[0], grad)
    pl.semaphore_wait(barrier, 3 + flag(x != 0) + flag(x >= 2) + jnp.where(last, 2 * NP, 2) + flag(relaying) + flag(relaying & (x == 1)))
    for k in range(NC):
        send_v(1, k)
    migrate(1)
    loads[4].wait()
    update_users(dot3(gap, vsplit, NN))
    for s in range(STRATA - 1, 0, -1):
        kt[s - 1] = kraw[:, s * R : (s + 1) * R].astype(jnp.float32).T
        if s == STRATA - 1:
            @pl.when(last)
            def _():
                send_far(3)

    for s in range(1, STRATA):
        ends = s == STRATA - 1
        for k in range(NC):
            v_copy(s, k).wait_recv()
            items = vin[s - 1, rows(k)]
            items_split = split(items)
            vh[rows(k)], vl[rows(k)] = items_split
            usplit = (uh[...], ul[...])
            gap = split(weigh(kt[s - 1, rows(k)], dot3(items_split, usplit, NT)))
            gh[rows(k)], gl[rows(k)] = gap
            gout[s - 1, rows(k)] = 2.0 * dot3(gap, usplit, NN) + (2.0 * ridge_weight) * items
            if ends:
                @pl.when(jnp.logical_not(last))
                def _():
                    f_copy(2, k).start()

                if k < 2:
                    pass_on(((2,), (0, 1))[k])
            else:
                g_copy(s, k).start()
        grad = dot3((gh[...], gl[...]), (vh[...], vl[...]), TN)
        if ends:
            user_grad[...] = user_gradient(grad)
            break
        update_users(grad)
        if s == STRATA - 2:
            stores = [pltpu.make_async_copy(users, u_out, store.at[0]), pltpu.make_async_copy(user_acc, a_out, store.at[1])]
            for copy in stores:
                copy.start()

            @pl.when(last)
            def _():
                send_far(2)
        for k in range(NC):
            @pl.when(x == XS - s)
            def _():
                m_copy(0, k).wait_recv()
                m_copy(1, k).wait_recv()

            @pl.when(x != XS - s)
            def _():
                v_copy(s, k).wait_send()

            g_copy(s, k).wait_recv()
            now = slot(s)
            home_v[now, rows(k)], home_b[now, rows(k)] = adagrad(home_v[now, rows(k)], home_b[now, rows(k)], gin[s - 1, rows(k)])
            send_v(s + 1, k)
        if s == STRATA - 2:
            @pl.when(last)
            def _():
                send_far(0)
                send_far(1)

            @pl.when(jnp.logical_not(last))
            def _():
                for k in range(NC):
                    f_copy(0, k).start()
                    f_copy(1, k).start()
        else:
            migrate(s + 1)
            pass_on((3,))
    stores.append(pltpu.make_async_copy(user_grad, e_out, store.at[2]))
    stores[2].start()

    @pl.when(first)
    def _():
        for p in range(NP):
            for which in range(4):
                last_leg(which, p).wait_recv()
        copies = [pltpu.make_async_copy(far.at[0], v_out, far_store.at[0]), pltpu.make_async_copy(far.at[1], b_out, far_store.at[1])]
        for copy in copies:
            copy.start()
        items, usplit = far[0], split(far[2])
        gap = split(weigh(far[3], dot3(split(items), usplit, NT)))
        far_grad[...] = 2.0 * dot3(gap, usplit, NN) + (2.0 * ridge_weight) * items
        copies.append(pltpu.make_async_copy(far_grad, g_out, far_store.at[2]))
        copies[2].start()
        for copy in copies:
            copy.wait()

    for which in range(4):
        @pl.when(relaying)
        def _():
            last_leg(which, 0).wait_send()

        @pl.when(last)
        def _():
            for p in range(NP):
                first_leg(which, p).wait_send()

    for s in range(1, STRATA):
        for k in range(NC):
            if s < STRATA - 1:
                g_copy(s, k).wait_send()

                @pl.when(x == XS - s)
                def _():
                    v_copy(s, k).wait_send()
            else:
                v_copy(s, k).wait_send()

    @pl.when(x >= 2)
    def _():
        for which in range(2):
            for k in range(NC):
                m_copy(which, k).wait_send()

    for which in range(3):
        for k in range(NC):
            @pl.when(jnp.logical_not(last))
            def _():
                f_copy(which, k).wait_send()

            @pl.when(jnp.logical_not(first))
            def _():
                f_copy(which, k).wait_recv()
    for copy in stores:
        copy.wait()


def last_step(value, acc, grad):
    acc = acc + grad * grad
    return value - step_rate * grad / jnp.sqrt(acc), acc


def body(user_factors, user_state, item_factors, item_state, counts):
    anywhere = pl.BlockSpec(memory_space=pl.ANY)
    block = jax.ShapeDtypeStruct((R, R), jnp.float32)
    f32, bf16 = jnp.float32, jnp.bfloat16
    dma = pltpu.SemaphoreType.DMA
    users, user_acc, user_grad, items, item_acc, item_grad = pl.pallas_call(
        functools.partial(kernel, lax.axis_size("blk"), lax.axis_size("group")),
        out_shape=(block,) * 6,
        in_specs=[anywhere] * 5,
        out_specs=(anywhere,) * 6,
        scratch_shapes=[
            pltpu.VMEM((R, R), f32), pltpu.VMEM((R, R), f32), pltpu.VMEM((R, R), f32),
            pltpu.VMEM((2, R, R), f32), pltpu.VMEM((2, R, R), f32),
            pltpu.VMEM((R, STRATA * R), jnp.int32), pltpu.VMEM((3, R, R), f32),
            pltpu.VMEM((3, R, R), f32), pltpu.VMEM((2, R, R), f32), pltpu.VMEM((3, R, R), f32),
            pltpu.VMEM((R, R), bf16), pltpu.VMEM((R, R), bf16),
            pltpu.VMEM((R, R), bf16), pltpu.VMEM((R, R), bf16),
            pltpu.VMEM((R, R), bf16), pltpu.VMEM((R, R), bf16),
            pltpu.VMEM((4, PIECE, R), f32), pltpu.VMEM((4, R, R), f32), pltpu.VMEM((R, R), f32),
            dma((5,)), dma((3,)),
            dma((3, NC)), dma((3, NC)), dma((2, NC)), dma((2, NC)),
            dma((2, NC)), dma((2, NC)), dma((3, NC)), dma((3, NC)), dma((4,)), dma((4,)), dma((4, NP)), dma((4, NP)), dma((3,)),
        ],
        compiler_params=pltpu.CompilerParams(collective_id=0, has_side_effects=True, vmem_limit_bytes=60 * 2**20),
        name="strata",
    )(user_factors, user_state, item_factors, item_state, counts)
    return last_step(users, user_acc, user_grad) + last_step(items, item_acc, item_grad)


def solution(mesh):
    spec = P(("blk", "group"), None)
    return jax.shard_map(body, mesh=mesh, in_specs=(spec,) * 5, out_specs=(spec,) * 4, check_vma=False)
```

```python
import functools
import jax
import jax.numpy as jnp
from jax import lax
from jax.experimental import pallas as pl
from jax.experimental.pallas import tpu as pltpu
from jax.sharding import PartitionSpec as P

STRATA = 4
R = 256
XS = 4
YC = 16
NC = 4
CH = R // NC
LANES = (1, 3, 5, 7, 9, 11, 13, 14)
NP = len(LANES)
PIECE = R // NP
MESH = pl.DeviceIdType.MESH

conf_scale = 0.5
ridge_weight = 0.01
step_rate = 0.1

NT = (((1,), (1,)), ((), ()))
NN = (((1,), (0,)), ((), ()))
TN = (((0,), (0,)), ((), ()))


def split(value):
    high = value.astype(jnp.bfloat16)
    return high, (value - high.astype(jnp.float32)).astype(jnp.bfloat16)


def dot3(left, right, dims):
    (lh, ll), (rh, rl) = left, right
    dot = functools.partial(lax.dot_general, dimension_numbers=dims, preferred_element_type=jnp.float32)
    return dot(lh, rh) + (dot(lh, rl) + dot(ll, rh))


def weigh(counts, predicted):
    prefer = (counts > 0).astype(jnp.float32)
    return (1.0 + conf_scale * counts) * (predicted - prefer)


def adagrad(value, acc, grad):
    acc = acc + grad * grad
    return value - step_rate * grad * lax.rsqrt(acc), acc


def kernel(n_blk, n_group, u_in, a_in, v_in, b_in, k_in, u_out, a_out, e_out, v_out, b_out, g_out,
           users, user_acc, user_grad, home_v, home_b, kraw, kt, vin, gin, gout, uh, ul, vh, vl, gh, gl, relay, far, far_grad,
           load, store, vsend, vrecv, gsend, grecv, msend, mrecv, fsend, frecv, asend, arecv, zsend, zrecv, far_store, hsend):
    b, g = lax.axis_index("blk"), lax.axis_index("group")
    x = lax.rem(b, XS)
    plane = b - x
    low, high = b < XS, b >= n_blk - XS

    def at(blk, group=g):
        return {"blk": blk, "group": group}

    def moved(blk_steps, group_steps=0):
        return at(lax.rem(b + blk_steps + n_blk, n_blk), lax.rem(g + group_steps + n_group, n_group))

    def ring(steps):
        return at(plane + lax.rem(x + steps, XS))

    def flag(condition):
        return condition.astype(jnp.int32)

    nxt, prv = moved(XS), moved(-XS)
    gone = jnp.where(x <= 1, XS, 0)
    lane = lax.rem(g, YC)
    first, last = lane == 0, lane == YC - 1
    relays = [lane == other for other in LANES]
    relaying = functools.reduce(jnp.logical_or, relays)

    loads = [
        pltpu.make_async_copy(u_in, users, load.at[0]),
        pltpu.make_async_copy(v_in, home_v.at[0], load.at[1]),
        pltpu.make_async_copy(k_in, kraw, load.at[2]),
        pltpu.make_async_copy(b_in, home_b.at[0], load.at[3]),
        pltpu.make_async_copy(a_in, user_acc, load.at[4]),
    ]
    for copy in loads:
        copy.start()

    barrier = pltpu.get_barrier_semaphore()

    def greet(*devices):
        for device in devices:
            pl.semaphore_signal(barrier, inc=1, device_id=device, device_id_type=MESH)

    greet(ring(1), ring(2), ring(3))

    @pl.when(x == 0)
    def _():
        greet(moved(1 - XS), moved(2 - XS), moved(3 - XS))

    @pl.when(x >= 2)
    def _():
        greet(prv)

    @pl.when(jnp.logical_not(first))
    def _():
        greet(moved(-gone, -1), moved(-1, -1))

    @pl.when(first)
    def _():
        greet(*[moved(-gone, other - YC) for other in LANES])

    @pl.when(first & (x == 1) & low)
    def _():
        greet(*[moved(-gone, other) for other in LANES])

    far_user = YC - 1 - lane + jnp.where((x == 1) & high, YC, 0)

    @pl.when(relaying)
    def _():
        greet(moved(0, YC - 1 - lane), moved(gone - 1, far_user))

    def rows(k):
        return pl.ds(k * CH, CH)

    def slot(s):
        return flag(x >= XS - s)

    def remote(src, dst, send, recv, device):
        return pltpu.make_async_remote_copy(src, dst, send, recv, device_id=device, device_id_type=MESH)

    def v_copy(s, k, device=None):
        return remote(home_v.at[slot(s - 1), rows(k)], vin.at[s - 1, rows(k)], vsend.at[s - 1, k], vrecv.at[s - 1, k],
                      ring(s) if device is None else device)

    def g_copy(s, k):
        return remote(gout.at[s - 1, rows(k)], gin.at[s - 1, rows(k)], gsend.at[s - 1, k], grecv.at[s - 1, k], ring(XS - s))

    def m_copy(which, k):
        ref = (home_v, home_b)[which]
        return remote(ref.at[0, rows(k)], ref.at[1, rows(k)], msend.at[which, k], mrecv.at[which, k], nxt)

    def home_rows(which, k):
        return (home_v, home_b)[which].at[slot(2), rows(k)]

    def steps(which):
        return 1 if which >= 2 else gone

    def f_copy(which, k):
        src = gout.at[2, rows(k)] if which == 2 else home_rows(which, k)
        return remote(src, (v_out, b_out, g_out)[which].at[rows(k)], fsend.at[which, k], frecv.at[which, k],
                      moved(steps(which), 1))

    def part(p):
        return pl.ds(p * PIECE, PIECE)

    def hand_on(k):
        return remote(vin.at[2, rows(k)], v_out.at[rows(k)], hsend.at[k], frecv.at[0, k], moved(1, 1))

    def first_leg(which, p):
        src = ((home_v, home_b)[which].at[slot(2), part(p)] if which < 2 else
               users.at[part(p)] if which == 2 else kt.at[2, part(p)])
        there = (moved(0, LANES[p] - YC + 1) if which < 2 else
                 moved(jnp.where((x == 0) | (x == XS - 1), 1 - XS, 1), LANES[p] - YC + 1 + jnp.where((x == 0) & low, YC, 0)))
        return remote(src, relay.at[which], zsend.at[which, p], arecv.at[which], there)

    def last_leg(which, p):
        return remote(relay.at[which], far.at[which, part(p)], asend.at[which], zrecv.at[which, p],
                      moved(gone, YC - LANES[p] - (0 if which < 2 else jnp.where((x == 1) & high, YC, 0))))

    def send_far(which):
        for p in range(NP):
            first_leg(which, p).start()

    def pass_on(arrays):
        for role, p in zip(relays, range(NP)):
            @pl.when(role)
            def _():
                for which in arrays:
                    first_leg(which, p).wait_recv()
                    last_leg(which, p).start()

    def send_v(s, k):
        @pl.when(x == XS - s)
        def _():
            v_copy(s, k, moved(s)).start()

        @pl.when(x != XS - s)
        def _():
            v_copy(s, k).start()

    def migrate(s):
        @pl.when(x == XS - s)
        def _():
            for k in range(NC):
                m_copy(0, k).start()
                m_copy(1, k).start()

    def user_gradient(grad):
        return 2.0 * grad + (2.0 * ridge_weight) * users[...]

    def update_users(grad):
        users[...], user_acc[...] = adagrad(users[...], user_acc[...], user_gradient(grad))
        uh[...], ul[...] = split(users[...])

    loads[0].wait()
    uh[...], ul[...] = split(users[...])
    loads[1].wait()
    usplit, grad = (uh[...], ul[...]), 0.0
    for h in range(2):
        half = pl.ds(h * R // 2, R // 2)
        items = home_v[0, half]
        items_split = split(items)
        if h == 0:
            loads[2].wait()
        gap = split(weigh(kraw[:, half].astype(jnp.float32), dot3(usplit, items_split, NT)))
        item_grad = 2.0 * dot3(gap, usplit, TN) + (2.0 * ridge_weight) * items
        if h == 0:
            loads[3].wait()
        home_v[0, half], home_b[0, half] = adagrad(items, home_b[0, half], item_grad)
        if h == 0:
            pl.semaphore_wait(barrier, 3 + flag(x != 0) + flag(x >= 2) + jnp.where(last, 2 * NP, 2) + flag(relaying) + flag(relaying & (x == 1) & high))
        for k in range(h * NC // 2, (h + 1) * NC // 2):
            send_v(1, k)
        grad = grad + dot3(gap, items_split, NN)
    migrate(1)
    loads[4].wait()
    update_users(grad)
    for s in range(STRATA - 1, 0, -1):
        kt[s - 1] = kraw[:, s * R : (s + 1) * R].astype(jnp.float32).T
        if s == STRATA - 1:
            @pl.when(last)
            def _():
                send_far(3)

    for s in range(1, STRATA):
        ends = s == STRATA - 1
        for k in range(NC):
            v_copy(s, k).wait_recv()
            if ends:
                @pl.when(jnp.logical_not(last) & (x == 0))
                def _():
                    hand_on(k).start()
            items = vin[s - 1, rows(k)]
            items_split = split(items)
            vh[rows(k)], vl[rows(k)] = items_split
            usplit = (uh[...], ul[...])
            gap = split(weigh(kt[s - 1, rows(k)], dot3(items_split, usplit, NT)))
            gh[rows(k)], gl[rows(k)] = gap
            gout[s - 1, rows(k)] = 2.0 * dot3(gap, usplit, NN) + (2.0 * ridge_weight) * items
            if ends:
                @pl.when(jnp.logical_not(last))
                def _():
                    f_copy(2, k).start()

                if k == 0:
                    pass_on((0, 1))

                    @pl.when(x == 1)
                    def _():
                        pass_on((2,))
                if k == 2:
                    @pl.when(jnp.logical_not(last) & (x == 0))
                    def _():
                        for w in range(2 * NC):
                            f_copy(w // NC, w % NC).start()
            else:
                g_copy(s, k).start()
        grad = dot3((gh[...], gl[...]), (vh[...], vl[...]), TN)
        if ends:
            user_grad[...] = user_gradient(grad)
            break
        update_users(grad)
        if s == STRATA - 2:
            stores = [pltpu.make_async_copy(users, u_out, store.at[0]), pltpu.make_async_copy(user_acc, a_out, store.at[1])]
            for copy in stores:
                copy.start()

            @pl.when(last)
            def _():
                send_far(2)
        for k in range(NC):
            @pl.when(x == XS - s)
            def _():
                m_copy(0, k).wait_recv()
                m_copy(1, k).wait_recv()

            @pl.when(x != XS - s)
            def _():
                v_copy(s, k).wait_send()

            g_copy(s, k).wait_recv()
            now = slot(s)
            home_v[now, rows(k)], home_b[now, rows(k)] = adagrad(home_v[now, rows(k)], home_b[now, rows(k)], gin[s - 1, rows(k)])
            send_v(s + 1, k)
            if s == STRATA - 2:
                @pl.when(last)
                def _():
                    for p in range(k * NP // NC, (k + 1) * NP // NC):
                        first_leg(0, p).start()
                        first_leg(1, p).start()
        if s == STRATA - 2:
            @pl.when(jnp.logical_not(last) & (x == 1))
            def _():
                for k in range(NC):
                    f_copy(1, k).start()

            @pl.when(jnp.logical_not(last) & (x >= 2))
            def _():
                for k in range(NC):
                    f_copy(0, k).start()
                    f_copy(1, k).start()
            @pl.when(x != 1)
            def _():
                pass_on((2,))
        else:
            migrate(s + 1)
            pass_on((3,))
    stores.append(pltpu.make_async_copy(user_grad, e_out, store.at[2]))
    stores[2].start()

    @pl.when(first)
    def _():
        for p in range(NP):
            last_leg(2, p).wait_recv()
        usplit = split(far[2])
        copies = []
        for p in range(NP):
            for which in (3, 0, 1):
                last_leg(which, p).wait_recv()
            for which, out in ((0, v_out), (1, b_out)):
                copies.append(pltpu.make_async_copy(far.at[which, part(p)], out.at[part(p)], far_store.at[which, p]))
                copies[-1].start()
            items = far[0, part(p)]
            gap = split(weigh(far[3, part(p)], dot3(split(items), usplit, NT)))
            far_grad[part(p)] = 2.0 * dot3(gap, usplit, NN) + (2.0 * ridge_weight) * items
            copies.append(pltpu.make_async_copy(far_grad.at[part(p)], g_out.at[part(p)], far_store.at[2, p]))
            copies[-1].start()
        for copy in copies:
            copy.wait()

    for which in range(4):
        @pl.when(relaying)
        def _():
            last_leg(which, 0).wait_send()

        @pl.when(last)
        def _():
            for p in range(NP):
                first_leg(which, p).wait_send()

    for s in range(1, STRATA):
        for k in range(NC):
            if s < STRATA - 1:
                g_copy(s, k).wait_send()

                @pl.when(x == XS - s)
                def _():
                    v_copy(s, k).wait_send()
            else:
                v_copy(s, k).wait_send()

    @pl.when(x >= 2)
    def _():
        for which in range(2):
            for k in range(NC):
                m_copy(which, k).wait_send()

    for which in range(3):
        for k in range(NC):
            @pl.when(jnp.logical_not(last) & ((x != 1) | (which != 0)))
            def _():
                f_copy(which, k).wait_send()

            @pl.when(jnp.logical_not(first))
            def _():
                f_copy(which, k).wait_recv()
    @pl.when(jnp.logical_not(last) & (x == 0))
    def _():
        for k in range(NC):
            hand_on(k).wait_send()

    for copy in stores:
        copy.wait()


def last_step(value, acc, grad):
    acc = acc + grad * grad
    return value - step_rate * grad / jnp.sqrt(acc), acc


def body(user_factors, user_state, item_factors, item_state, counts):
    anywhere = pl.BlockSpec(memory_space=pl.ANY)
    block = jax.ShapeDtypeStruct((R, R), jnp.float32)
    f32, bf16 = jnp.float32, jnp.bfloat16
    dma = pltpu.SemaphoreType.DMA
    users, user_acc, user_grad, items, item_acc, item_grad = pl.pallas_call(
        functools.partial(kernel, lax.axis_size("blk"), lax.axis_size("group")),
        out_shape=(block,) * 6,
        in_specs=[anywhere] * 5,
        out_specs=(anywhere,) * 6,
        scratch_shapes=[
            pltpu.VMEM((R, R), f32), pltpu.VMEM((R, R), f32), pltpu.VMEM((R, R), f32),
            pltpu.VMEM((2, R, R), f32), pltpu.VMEM((2, R, R), f32),
            pltpu.VMEM((R, STRATA * R), jnp.int32), pltpu.VMEM((3, R, R), f32),
            pltpu.VMEM((3, R, R), f32), pltpu.VMEM((2, R, R), f32), pltpu.VMEM((3, R, R), f32),
            pltpu.VMEM((R, R), bf16), pltpu.VMEM((R, R), bf16),
            pltpu.VMEM((R, R), bf16), pltpu.VMEM((R, R), bf16),
            pltpu.VMEM((R, R), bf16), pltpu.VMEM((R, R), bf16),
            pltpu.VMEM((4, PIECE, R), f32), pltpu.VMEM((4, R, R), f32), pltpu.VMEM((R, R), f32),
            dma((5,)), dma((3,)),
            dma((3, NC)), dma((3, NC)), dma((2, NC)), dma((2, NC)),
            dma((2, NC)), dma((2, NC)), dma((3, NC)), dma((3, NC)), dma((4,)), dma((4,)), dma((4, NP)), dma((4, NP)), dma((3, NP)), dma((NC,)),
        ],
        compiler_params=pltpu.CompilerParams(collective_id=0, has_side_effects=True, vmem_limit_bytes=60 * 2**20),
        name="strata",
    )(user_factors, user_state, item_factors, item_state, counts)
    return last_step(users, user_acc, user_grad) + last_step(items, item_acc, item_grad)


def solution(mesh):
    spec = P(("blk", "group"), None)
    return jax.shard_map(body, mesh=mesh, in_specs=(spec,) * 5, out_specs=(spec,) * 4, check_vma=False)
```

```python
import functools
import jax
import jax.numpy as jnp
from jax import lax
from jax.experimental import pallas as pl
from jax.experimental.pallas import tpu as pltpu
from jax.sharding import PartitionSpec as P

STRATA = 4
R = 256
XS = 4
YC = 16
NC = 4
CH = R // NC
LANES = (1, 3, 5, 7, 9, 11, 13, 14)
NP = len(LANES)
PIECE = R // NP
MESH = pl.DeviceIdType.MESH

conf_scale = 0.5
ridge_weight = 0.01
step_rate = 0.1

NT = (((1,), (1,)), ((), ()))
NN = (((1,), (0,)), ((), ()))
TN = (((0,), (0,)), ((), ()))


def split(value):
    high = value.astype(jnp.bfloat16)
    return high, (value - high.astype(jnp.float32)).astype(jnp.bfloat16)


def dot3(left, right, dims):
    (lh, ll), (rh, rl) = left, right
    dot = functools.partial(lax.dot_general, dimension_numbers=dims, preferred_element_type=jnp.float32)
    return dot(lh, rh) + (dot(lh, rl) + dot(ll, rh))


def weigh(counts, predicted):
    prefer = (counts > 0).astype(jnp.float32)
    return (1.0 + conf_scale * counts) * (predicted - prefer)


def adagrad(value, acc, grad):
    acc = acc + grad * grad
    return value - step_rate * grad * lax.rsqrt(acc), acc


def kernel(n_blk, n_group, u_in, a_in, v_in, b_in, k_in, u_out, a_out, e_out, v_out, b_out, g_out,
           users, user_acc, user_grad, home_v, home_b, kraw, kt, vin, gin, gout, uh, ul, vh, vl, gh, gl, relay, far, far_grad,
           load, store, vsend, vrecv, gsend, grecv, msend, mrecv, fsend, frecv, asend, arecv, zsend, zrecv, far_store, hsend):
    b, g = lax.axis_index("blk"), lax.axis_index("group")
    x = lax.rem(b, XS)
    plane = b - x
    low, high = b < XS, b >= n_blk - XS

    def at(blk, group=g):
        return {"blk": blk, "group": group}

    def moved(blk_steps, group_steps=0):
        return at(lax.rem(b + blk_steps + n_blk, n_blk), lax.rem(g + group_steps + n_group, n_group))

    def ring(steps):
        return at(plane + lax.rem(x + steps, XS))

    def flag(condition):
        return condition.astype(jnp.int32)

    nxt, prv = moved(XS), moved(-XS)
    gone = jnp.where(x <= 1, XS, 0)
    lane = lax.rem(g, YC)
    first, last = lane == 0, lane == YC - 1
    relays = [lane == other for other in LANES]
    relaying = functools.reduce(jnp.logical_or, relays)

    loads = [
        pltpu.make_async_copy(u_in, users, load.at[0]),
        pltpu.make_async_copy(v_in, home_v.at[0], load.at[1]),
        pltpu.make_async_copy(k_in, kraw, load.at[2]),
        pltpu.make_async_copy(b_in, home_b.at[0], load.at[3]),
        pltpu.make_async_copy(a_in, user_acc, load.at[4]),
    ]
    for copy in loads:
        copy.start()

    barrier = pltpu.get_barrier_semaphore()

    def greet(*devices):
        for device in devices:
            pl.semaphore_signal(barrier, inc=1, device_id=device, device_id_type=MESH)

    greet(ring(1), ring(2), ring(3))

    @pl.when(x == 0)
    def _():
        greet(moved(1 - XS), moved(2 - XS), moved(3 - XS))

    @pl.when(x >= 2)
    def _():
        greet(prv)

    @pl.when(jnp.logical_not(first))
    def _():
        greet(moved(-gone, -1), moved(-1, -1))

    @pl.when(first)
    def _():
        greet(*[moved(-gone, other - YC) for other in LANES])

    @pl.when(first & (x == 1) & low)
    def _():
        greet(*[moved(-gone, other) for other in LANES])

    far_user = YC - 1 - lane + jnp.where((x == 1) & high, YC, 0)

    @pl.when(relaying)
    def _():
        greet(moved(0, YC - 1 - lane), moved(gone - 1, far_user))

    def rows(k):
        return pl.ds(k * CH, CH)

    def slot(s):
        return flag(x >= XS - s)

    def remote(src, dst, send, recv, device):
        return pltpu.make_async_remote_copy(src, dst, send, recv, device_id=device, device_id_type=MESH)

    def v_copy(s, k, device=None):
        return remote(home_v.at[slot(s - 1), rows(k)], vin.at[s - 1, rows(k)], vsend.at[s - 1, k], vrecv.at[s - 1, k],
                      ring(s) if device is None else device)

    def g_copy(s, k):
        return remote(gout.at[s - 1, rows(k)], gin.at[s - 1, rows(k)], gsend.at[s - 1, k], grecv.at[s - 1, k], ring(XS - s))

    def m_copy(which, k):
        ref = (home_v, home_b)[which]
        return remote(ref.at[0, rows(k)], ref.at[1, rows(k)], msend.at[which, k], mrecv.at[which, k], nxt)

    def home_rows(which, k):
        return (home_v, home_b)[which].at[slot(2), rows(k)]

    def steps(which):
        return 1 if which >= 2 else gone

    def f_copy(which, k):
        src = gout.at[2, rows(k)] if which == 2 else home_rows(which, k)
        return remote(src, (v_out, b_out, g_out)[which].at[rows(k)], fsend.at[which, k], frecv.at[which, k],
                      moved(steps(which), 1))

    def part(p):
        return pl.ds(p * PIECE, PIECE)

    later = jnp.logical_not(last) & (x <= 1) & (b < n_blk - XS)

    def send_state():
        for k in range(NC):
            @pl.when(x != 1)
            def _():
                f_copy(0, k).start()

            f_copy(1, k).start()

    def hand_on(k):
        return remote(vin.at[2, rows(k)], v_out.at[rows(k)], hsend.at[k], frecv.at[0, k], moved(1, 1))

    def first_leg(which, p):
        src = ((home_v, home_b)[which].at[slot(2), part(p)] if which < 2 else
               users.at[part(p)] if which == 2 else kt.at[2, part(p)])
        there = (moved(0, LANES[p] - YC + 1) if which < 2 else
                 moved(jnp.where((x == 0) | (x == XS - 1), 1 - XS, 1), LANES[p] - YC + 1 + jnp.where((x == 0) & low, YC, 0)))
        return remote(src, relay.at[which], zsend.at[which, p], arecv.at[which], there)

    def last_leg(which, p):
        return remote(relay.at[which], far.at[which, part(p)], asend.at[which], zrecv.at[which, p],
                      moved(gone, YC - LANES[p] - (0 if which < 2 else jnp.where((x == 1) & high, YC, 0))))

    def send_far(which):
        for p in range(NP):
            first_leg(which, p).start()

    def pass_on(arrays):
        for role, p in zip(relays, range(NP)):
            @pl.when(role)
            def _():
                for which in arrays:
                    first_leg(which, p).wait_recv()
                    last_leg(which, p).start()

    def send_v(s, k):
        @pl.when(x == XS - s)
        def _():
            v_copy(s, k, moved(s)).start()

        @pl.when(x != XS - s)
        def _():
            v_copy(s, k).start()

    def migrate(s):
        @pl.when(x == XS - s)
        def _():
            for k in range(NC):
                m_copy(0, k).start()
                m_copy(1, k).start()

    def user_gradient(grad):
        return 2.0 * grad + (2.0 * ridge_weight) * users[...]

    def update_users(grad):
        users[...], user_acc[...] = adagrad(users[...], user_acc[...], user_gradient(grad))
        uh[...], ul[...] = split(users[...])

    loads[0].wait()
    uh[...], ul[...] = split(users[...])
    loads[1].wait()
    usplit, grad = (uh[...], ul[...]), 0.0
    for h in range(2):
        half = pl.ds(h * R // 2, R // 2)
        items = home_v[0, half]
        items_split = split(items)
        if h == 0:
            loads[2].wait()
        gap = split(weigh(kraw[:, half].astype(jnp.float32), dot3(usplit, items_split, NT)))
        item_grad = 2.0 * dot3(gap, usplit, TN) + (2.0 * ridge_weight) * items
        if h == 0:
            loads[3].wait()
        home_v[0, half], home_b[0, half] = adagrad(items, home_b[0, half], item_grad)
        if h == 0:
            pl.semaphore_wait(barrier, 3 + flag(x != 0) + flag(x >= 2) + jnp.where(last, 2 * NP, 2) + flag(relaying) + flag(relaying & (x == 1) & high))
        for k in range(h * NC // 2, (h + 1) * NC // 2):
            send_v(1, k)
        grad = grad + dot3(gap, items_split, NN)
    migrate(1)
    loads[4].wait()
    update_users(grad)
    for s in range(STRATA - 1, 0, -1):
        kt[s - 1] = kraw[:, s * R : (s + 1) * R].astype(jnp.float32).T
        if s == STRATA - 1:
            @pl.when(last)
            def _():
                send_far(3)

    for s in range(1, STRATA):
        ends = s == STRATA - 1
        for k in range(NC):
            v_copy(s, k).wait_recv()
            if ends:
                @pl.when(jnp.logical_not(last) & (x == 0))
                def _():
                    hand_on(k).start()
            items = vin[s - 1, rows(k)]
            items_split = split(items)
            vh[rows(k)], vl[rows(k)] = items_split
            usplit = (uh[...], ul[...])
            gap = split(weigh(kt[s - 1, rows(k)], dot3(items_split, usplit, NT)))
            gh[rows(k)], gl[rows(k)] = gap
            gout[s - 1, rows(k)] = 2.0 * dot3(gap, usplit, NN) + (2.0 * ridge_weight) * items
            if ends:
                @pl.when(jnp.logical_not(last))
                def _():
                    f_copy(2, k).start()

                if k == 0:
                    pass_on((0, 1))

                    @pl.when(x == 1)
                    def _():
                        pass_on((2,))
                if k == 2:
                    @pl.when(later)
                    def _():
                        send_state()
            else:
                g_copy(s, k).start()
        grad = dot3((gh[...], gl[...]), (vh[...], vl[...]), TN)
        if ends:
            user_grad[...] = user_gradient(grad)
            break
        update_users(grad)
        if s == STRATA - 2:
            stores = [pltpu.make_async_copy(users, u_out, store.at[0]), pltpu.make_async_copy(user_acc, a_out, store.at[1])]
            for copy in stores:
                copy.start()

            @pl.when(last)
            def _():
                send_far(2)
        for k in range(NC):
            @pl.when(x == XS - s)
            def _():
                m_copy(0, k).wait_recv()
                m_copy(1, k).wait_recv()

            @pl.when(x != XS - s)
            def _():
                v_copy(s, k).wait_send()

            g_copy(s, k).wait_recv()
            now = slot(s)
            home_v[now, rows(k)], home_b[now, rows(k)] = adagrad(home_v[now, rows(k)], home_b[now, rows(k)], gin[s - 1, rows(k)])
            send_v(s + 1, k)
            if s == STRATA - 2:
                @pl.when(last)
                def _():
                    for p in range(k * NP // NC, (k + 1) * NP // NC):
                        first_leg(0, p).start()
                        first_leg(1, p).start()
        if s == STRATA - 2:
            @pl.when(jnp.logical_not(last | later))
            def _():
                send_state()
            @pl.when(x != 1)
            def _():
                pass_on((2,))
        else:
            migrate(s + 1)
            pass_on((3,))
    stores.append(pltpu.make_async_copy(user_grad, e_out, store.at[2]))
    stores[2].start()

    @pl.when(first)
    def _():
        for p in range(NP):
            last_leg(2, p).wait_recv()
        usplit = split(far[2])
        copies = []
        for p in range(NP):
            for which in (3, 0, 1):
                last_leg(which, p).wait_recv()
            for which, out in ((0, v_out), (1, b_out)):
                copies.append(pltpu.make_async_copy(far.at[which, part(p)], out.at[part(p)], far_store.at[which, p]))
                copies[-1].start()
            items = far[0, part(p)]
            gap = split(weigh(far[3, part(p)], dot3(split(items), usplit, NT)))
            far_grad[part(p)] = 2.0 * dot3(gap, usplit, NN) + (2.0 * ridge_weight) * items
            copies.append(pltpu.make_async_copy(far_grad.at[part(p)], g_out.at[part(p)], far_store.at[2, p]))
            copies[-1].start()
        for copy in copies:
            copy.wait()

    for which in range(4):
        @pl.when(relaying)
        def _():
            last_leg(which, 0).wait_send()

        @pl.when(last)
        def _():
            for p in range(NP):
                first_leg(which, p).wait_send()

    for s in range(1, STRATA):
        for k in range(NC):
            if s < STRATA - 1:
                g_copy(s, k).wait_send()

                @pl.when(x == XS - s)
                def _():
                    v_copy(s, k).wait_send()
            else:
                v_copy(s, k).wait_send()

    @pl.when(x >= 2)
    def _():
        for which in range(2):
            for k in range(NC):
                m_copy(which, k).wait_send()

    for which in range(3):
        for k in range(NC):
            @pl.when(jnp.logical_not(last) & ((x != 1) | (which != 0)))
            def _():
                f_copy(which, k).wait_send()

            @pl.when(jnp.logical_not(first))
            def _():
                f_copy(which, k).wait_recv()
    @pl.when(jnp.logical_not(last) & (x == 0))
    def _():
        for k in range(NC):
            hand_on(k).wait_send()

    for copy in stores:
        copy.wait()


def last_step(value, acc, grad):
    acc = acc + grad * grad
    return value - step_rate * grad / jnp.sqrt(acc), acc


def body(user_factors, user_state, item_factors, item_state, counts):
    anywhere = pl.BlockSpec(memory_space=pl.ANY)
    block = jax.ShapeDtypeStruct((R, R), jnp.float32)
    f32, bf16 = jnp.float32, jnp.bfloat16
    dma = pltpu.SemaphoreType.DMA
    users, user_acc, user_grad, items, item_acc, item_grad = pl.pallas_call(
        functools.partial(kernel, lax.axis_size("blk"), lax.axis_size("group")),
        out_shape=(block,) * 6,
        in_specs=[anywhere] * 5,
        out_specs=(anywhere,) * 6,
        scratch_shapes=[
            pltpu.VMEM((R, R), f32), pltpu.VMEM((R, R), f32), pltpu.VMEM((R, R), f32),
            pltpu.VMEM((2, R, R), f32), pltpu.VMEM((2, R, R), f32),
            pltpu.VMEM((R, STRATA * R), jnp.int32), pltpu.VMEM((3, R, R), f32),
            pltpu.VMEM((3, R, R), f32), pltpu.VMEM((2, R, R), f32), pltpu.VMEM((3, R, R), f32),
            pltpu.VMEM((R, R), bf16), pltpu.VMEM((R, R), bf16),
            pltpu.VMEM((R, R), bf16), pltpu.VMEM((R, R), bf16),
            pltpu.VMEM((R, R), bf16), pltpu.VMEM((R, R), bf16),
            pltpu.VMEM((4, PIECE, R), f32), pltpu.VMEM((4, R, R), f32), pltpu.VMEM((R, R), f32),
            dma((5,)), dma((3,)),
            dma((3, NC)), dma((3, NC)), dma((2, NC)), dma((2, NC)),
            dma((2, NC)), dma((2, NC)), dma((3, NC)), dma((3, NC)), dma((4,)), dma((4,)), dma((4, NP)), dma((4, NP)), dma((3, NP)), dma((NC,)),
        ],
        compiler_params=pltpu.CompilerParams(collective_id=0, has_side_effects=True, vmem_limit_bytes=60 * 2**20),
        name="strata",
    )(user_factors, user_state, item_factors, item_state, counts)
    return last_step(users, user_acc, user_grad) + last_step(items, item_acc, item_grad)


def solution(mesh):
    spec = P(("blk", "group"), None)
    return jax.shard_map(body, mesh=mesh, in_specs=(spec,) * 5, out_specs=(spec,) * 4, check_vma=False)
```

```python
import functools
import jax
import jax.numpy as jnp
from jax import lax
from jax.experimental import pallas as pl
from jax.experimental.pallas import tpu as pltpu
from jax.sharding import PartitionSpec as P

STRATA = 4
R = 256
XS = 4
YC = 16
NC = 4
CH = R // NC
LANES = (1, 3, 5, 7, 9, 11, 13, 14)
NP = len(LANES)
PIECE = R // NP
MESH = pl.DeviceIdType.MESH

conf_scale = 0.5
ridge_weight = 0.01
step_rate = 0.1

NT = (((1,), (1,)), ((), ()))
NN = (((1,), (0,)), ((), ()))
TN = (((0,), (0,)), ((), ()))


def split(value):
    high = value.astype(jnp.bfloat16)
    return high, (value - high.astype(jnp.float32)).astype(jnp.bfloat16)


def dot3(left, right, dims):
    (lh, ll), (rh, rl) = left, right
    dot = functools.partial(lax.dot_general, dimension_numbers=dims, preferred_element_type=jnp.float32)
    return dot(lh, rh) + (dot(lh, rl) + dot(ll, rh))


def weigh(counts, predicted):
    prefer = (counts > 0).astype(jnp.float32)
    return (1.0 + conf_scale * counts) * (predicted - prefer)


def adagrad(value, acc, grad):
    acc = acc + grad * grad
    return value - step_rate * grad * lax.rsqrt(acc), acc


def kernel(n_blk, n_group, u_in, a_in, v_in, b_in, k_in, u_out, a_out, e_out, v_out, b_out, g_out,
           users, user_acc, user_grad, home_v, home_b, kraw, kt, vin, gin, gout, uh, ul, vh, vl, gh, gl, relay, far, far_grad,
           load, store, vsend, vrecv, gsend, grecv, msend, mrecv, fsend, frecv, asend, arecv, zsend, zrecv, far_store, hsend):
    b, g = lax.axis_index("blk"), lax.axis_index("group")
    x = lax.rem(b, XS)
    plane = b - x
    low, high = b < XS, b >= n_blk - XS

    def at(blk, group=g):
        return {"blk": blk, "group": group}

    def moved(blk_steps, group_steps=0):
        return at(lax.rem(b + blk_steps + n_blk, n_blk), lax.rem(g + group_steps + n_group, n_group))

    def ring(steps):
        return at(plane + lax.rem(x + steps, XS))

    def flag(condition):
        return condition.astype(jnp.int32)

    nxt, prv = moved(XS), moved(-XS)
    gone = jnp.where(x <= 1, XS, 0)
    lane = lax.rem(g, YC)
    first, last = lane == 0, lane == YC - 1
    relays = [lane == other for other in LANES]
    relaying = functools.reduce(jnp.logical_or, relays)

    loads = [
        pltpu.make_async_copy(u_in, users, load.at[0]),
        pltpu.make_async_copy(v_in, home_v.at[0], load.at[1]),
        pltpu.make_async_copy(k_in.at[:, pl.ds(0, R)], kraw.at[:, pl.ds(0, R)], load.at[2]),
        pltpu.make_async_copy(b_in, home_b.at[0], load.at[3]),
        pltpu.make_async_copy(a_in, user_acc, load.at[4]),
        pltpu.make_async_copy(k_in.at[:, pl.ds(R, 3 * R)], kraw.at[:, pl.ds(R, 3 * R)], load.at[5]),
    ]
    for copy in loads:
        copy.start()

    barrier = pltpu.get_barrier_semaphore()

    def greet(*devices):
        for device in devices:
            pl.semaphore_signal(barrier, inc=1, device_id=device, device_id_type=MESH)

    greet(ring(1), ring(2), ring(3))

    @pl.when(x == 0)
    def _():
        greet(moved(1 - XS), moved(2 - XS), moved(3 - XS))

    @pl.when(x >= 2)
    def _():
        greet(prv)

    @pl.when(jnp.logical_not(first))
    def _():
        greet(moved(-gone, -1), moved(-1, -1))

    @pl.when(first)
    def _():
        greet(*[moved(-gone, other - YC) for other in LANES])

    @pl.when(first & (x == 1) & low)
    def _():
        greet(*[moved(-gone, other) for other in LANES])

    far_user = YC - 1 - lane + jnp.where((x == 1) & high, YC, 0)

    @pl.when(relaying)
    def _():
        greet(moved(0, YC - 1 - lane), moved(gone - 1, far_user))

    def rows(k):
        return pl.ds(k * CH, CH)

    def slot(s):
        return flag(x >= XS - s)

    def remote(src, dst, send, recv, device):
        return pltpu.make_async_remote_copy(src, dst, send, recv, device_id=device, device_id_type=MESH)

    def v_copy(s, k, device=None):
        return remote(home_v.at[slot(s - 1), rows(k)], vin.at[s - 1, rows(k)], vsend.at[s - 1, k], vrecv.at[s - 1, k],
                      ring(s) if device is None else device)

    def g_copy(s, k):
        return remote(gout.at[s - 1, rows(k)], gin.at[s - 1, rows(k)], gsend.at[s - 1, k], grecv.at[s - 1, k], ring(XS - s))

    def m_copy(which, k):
        ref = (home_v, home_b)[which]
        return remote(ref.at[0, rows(k)], ref.at[1, rows(k)], msend.at[which, k], mrecv.at[which, k], nxt)

    def home_rows(which, k):
        return (home_v, home_b)[which].at[slot(2), rows(k)]

    def steps(which):
        return 1 if which >= 2 else gone

    def f_copy(which, k):
        src = gout.at[2, rows(k)] if which == 2 else home_rows(which, k)
        return remote(src, (v_out, b_out, g_out)[which].at[rows(k)], fsend.at[which, k], frecv.at[which, k],
                      moved(steps(which), 1))

    def part(p):
        return pl.ds(p * PIECE, PIECE)

    later = jnp.logical_not(last) & (x <= 1) & (b < n_blk - XS)

    def send_state():
        for k in range(NC):
            @pl.when(x != 1)
            def _():
                f_copy(0, k).start()

            f_copy(1, k).start()

    def hand_on(k):
        return remote(vin.at[2, rows(k)], v_out.at[rows(k)], hsend.at[k], frecv.at[0, k], moved(1, 1))

    def first_leg(which, p):
        src = ((home_v, home_b)[which].at[slot(2), part(p)] if which < 2 else
               users.at[part(p)] if which == 2 else kt.at[2, part(p)])
        there = (moved(0, LANES[p] - YC + 1) if which < 2 else
                 moved(jnp.where((x == 0) | (x == XS - 1), 1 - XS, 1), LANES[p] - YC + 1 + jnp.where((x == 0) & low, YC, 0)))
        return remote(src, relay.at[which], zsend.at[which, p], arecv.at[which], there)

    def last_leg(which, p):
        return remote(relay.at[which], far.at[which, part(p)], asend.at[which], zrecv.at[which, p],
                      moved(gone, YC - LANES[p] - (0 if which < 2 else jnp.where((x == 1) & high, YC, 0))))

    def send_far(which):
        for p in range(NP):
            first_leg(which, p).start()

    def pass_on(arrays):
        for role, p in zip(relays, range(NP)):
            @pl.when(role)
            def _():
                for which in arrays:
                    first_leg(which, p).wait_recv()
                    last_leg(which, p).start()

    def send_v(s, k):
        @pl.when(x == XS - s)
        def _():
            v_copy(s, k, moved(s)).start()

        @pl.when(x != XS - s)
        def _():
            v_copy(s, k).start()

    def migrate(s):
        @pl.when(x == XS - s)
        def _():
            for k in range(NC):
                m_copy(0, k).start()
                m_copy(1, k).start()

    def user_gradient(grad):
        return 2.0 * grad + (2.0 * ridge_weight) * users[...]

    def update_users(grad):
        users[...], user_acc[...] = adagrad(users[...], user_acc[...], user_gradient(grad))
        uh[...], ul[...] = split(users[...])

    loads[0].wait()
    uh[...], ul[...] = split(users[...])
    loads[1].wait()
    usplit, grad = (uh[...], ul[...]), 0.0
    for h in range(2):
        half = pl.ds(h * R // 2, R // 2)
        items = home_v[0, half]
        items_split = split(items)
        if h == 0:
            loads[2].wait()
        gap = split(weigh(kraw[:, half].astype(jnp.float32), dot3(usplit, items_split, NT)))
        item_grad = 2.0 * dot3(gap, usplit, TN) + (2.0 * ridge_weight) * items
        if h == 0:
            loads[3].wait()
        home_v[0, half], home_b[0, half] = adagrad(items, home_b[0, half], item_grad)
        if h == 0:
            pl.semaphore_wait(barrier, 3 + flag(x != 0) + flag(x >= 2) + jnp.where(last, 2 * NP, 2) + flag(relaying) + flag(relaying & (x == 1) & high))
        for k in range(h * NC // 2, (h + 1) * NC // 2):
            send_v(1, k)
        grad = grad + dot3(gap, items_split, NN)
    migrate(1)
    loads[4].wait()
    update_users(grad)
    loads[5].wait()
    for s in range(STRATA - 1, 0, -1):
        kt[s - 1] = kraw[:, s * R : (s + 1) * R].astype(jnp.float32).T
        if s == STRATA - 1:
            @pl.when(last)
            def _():
                send_far(3)

    for s in range(1, STRATA):
        ends = s == STRATA - 1
        for k in range(NC):
            v_copy(s, k).wait_recv()
            if ends:
                @pl.when(jnp.logical_not(last) & (x == 0))
                def _():
                    hand_on(k).start()
            items = vin[s - 1, rows(k)]
            items_split = split(items)
            vh[rows(k)], vl[rows(k)] = items_split
            usplit = (uh[...], ul[...])
            gap = split(weigh(kt[s - 1, rows(k)], dot3(items_split, usplit, NT)))
            gh[rows(k)], gl[rows(k)] = gap
            gout[s - 1, rows(k)] = 2.0 * dot3(gap, usplit, NN) + (2.0 * ridge_weight) * items
            if ends:
                @pl.when(jnp.logical_not(last))
                def _():
                    f_copy(2, k).start()

                if k == 0:
                    pass_on((0, 1))

                    @pl.when(x == 1)
                    def _():
                        pass_on((2,))
                if k == 2:
                    @pl.when(later)
                    def _():
                        send_state()
            else:
                g_copy(s, k).start()
        grad = dot3((gh[...], gl[...]), (vh[...], vl[...]), TN)
        if ends:
            user_grad[...] = user_gradient(grad)
            break
        update_users(grad)
        if s == STRATA - 2:
            stores = [pltpu.make_async_copy(users, u_out, store.at[0]), pltpu.make_async_copy(user_acc, a_out, store.at[1])]
            for copy in stores:
                copy.start()

            @pl.when(last)
            def _():
                send_far(2)
        for k in range(NC):
            @pl.when(x == XS - s)
            def _():
                m_copy(0, k).wait_recv()
                m_copy(1, k).wait_recv()

            @pl.when(x != XS - s)
            def _():
                v_copy(s, k).wait_send()

            g_copy(s, k).wait_recv()
            now = slot(s)
            home_v[now, rows(k)], home_b[now, rows(k)] = adagrad(home_v[now, rows(k)], home_b[now, rows(k)], gin[s - 1, rows(k)])
            send_v(s + 1, k)
            if s == STRATA - 2:
                @pl.when(last)
                def _():
                    for p in range(k * NP // NC, (k + 1) * NP // NC):
                        first_leg(0, p).start()
                        first_leg(1, p).start()
        if s == STRATA - 2:
            @pl.when(jnp.logical_not(last | later))
            def _():
                send_state()
            @pl.when(x != 1)
            def _():
                pass_on((2,))
        else:
            migrate(s + 1)
            pass_on((3,))
    stores.append(pltpu.make_async_copy(user_grad, e_out, store.at[2]))
    stores[2].start()

    @pl.when(first)
    def _():
        for p in range(NP):
            last_leg(2, p).wait_recv()
        usplit = split(far[2])
        copies = []
        for p in range(NP):
            for which in (3, 0, 1):
                last_leg(which, p).wait_recv()
            for which, out in ((0, v_out), (1, b_out)):
                copies.append(pltpu.make_async_copy(far.at[which, part(p)], out.at[part(p)], far_store.at[which, p]))
                copies[-1].start()
            items = far[0, part(p)]
            gap = split(weigh(far[3, part(p)], dot3(split(items), usplit, NT)))
            far_grad[part(p)] = 2.0 * dot3(gap, usplit, NN) + (2.0 * ridge_weight) * items
            copies.append(pltpu.make_async_copy(far_grad.at[part(p)], g_out.at[part(p)], far_store.at[2, p]))
            copies[-1].start()
        for copy in copies:
            copy.wait()

    for which in range(4):
        @pl.when(relaying)
        def _():
            last_leg(which, 0).wait_send()

        @pl.when(last)
        def _():
            for p in range(NP):
                first_leg(which, p).wait_send()

    for s in range(1, STRATA):
        for k in range(NC):
            if s < STRATA - 1:
                g_copy(s, k).wait_send()

                @pl.when(x == XS - s)
                def _():
                    v_copy(s, k).wait_send()
            else:
                v_copy(s, k).wait_send()

    @pl.when(x >= 2)
    def _():
        for which in range(2):
            for k in range(NC):
                m_copy(which, k).wait_send()

    for which in range(3):
        for k in range(NC):
            @pl.when(jnp.logical_not(last) & ((x != 1) | (which != 0)))
            def _():
                f_copy(which, k).wait_send()

            @pl.when(jnp.logical_not(first))
            def _():
                f_copy(which, k).wait_recv()
    @pl.when(jnp.logical_not(last) & (x == 0))
    def _():
        for k in range(NC):
            hand_on(k).wait_send()

    for copy in stores:
        copy.wait()


def last_step(value, acc, grad):
    acc = acc + grad * grad
    return value - step_rate * grad / jnp.sqrt(acc), acc


def body(user_factors, user_state, item_factors, item_state, counts):
    anywhere = pl.BlockSpec(memory_space=pl.ANY)
    block = jax.ShapeDtypeStruct((R, R), jnp.float32)
    f32, bf16 = jnp.float32, jnp.bfloat16
    dma = pltpu.SemaphoreType.DMA
    users, user_acc, user_grad, items, item_acc, item_grad = pl.pallas_call(
        functools.partial(kernel, lax.axis_size("blk"), lax.axis_size("group")),
        out_shape=(block,) * 6,
        in_specs=[anywhere] * 5,
        out_specs=(anywhere,) * 6,
        scratch_shapes=[
            pltpu.VMEM((R, R), f32), pltpu.VMEM((R, R), f32), pltpu.VMEM((R, R), f32),
            pltpu.VMEM((2, R, R), f32), pltpu.VMEM((2, R, R), f32),
            pltpu.VMEM((R, STRATA * R), jnp.int32), pltpu.VMEM((3, R, R), f32),
            pltpu.VMEM((3, R, R), f32), pltpu.VMEM((2, R, R), f32), pltpu.VMEM((3, R, R), f32),
            pltpu.VMEM((R, R), bf16), pltpu.VMEM((R, R), bf16),
            pltpu.VMEM((R, R), bf16), pltpu.VMEM((R, R), bf16),
            pltpu.VMEM((R, R), bf16), pltpu.VMEM((R, R), bf16),
            pltpu.VMEM((4, PIECE, R), f32), pltpu.VMEM((4, R, R), f32), pltpu.VMEM((R, R), f32),
            dma((6,)), dma((3,)),
            dma((3, NC)), dma((3, NC)), dma((2, NC)), dma((2, NC)),
            dma((2, NC)), dma((2, NC)), dma((3, NC)), dma((3, NC)), dma((4,)), dma((4,)), dma((4, NP)), dma((4, NP)), dma((3, NP)), dma((NC,)),
        ],
        compiler_params=pltpu.CompilerParams(collective_id=0, has_side_effects=True, vmem_limit_bytes=60 * 2**20),
        name="strata",
    )(user_factors, user_state, item_factors, item_state, counts)
    return last_step(users, user_acc, user_grad) + last_step(items, item_acc, item_grad)


def solution(mesh):
    spec = P(("blk", "group"), None)
    return jax.shard_map(body, mesh=mesh, in_specs=(spec,) * 5, out_specs=(spec,) * 4, check_vma=False)
```
